512 devices in a mesh: cls: 32 (over z, core), pen: 16 (over x, y).
Axes of the slice: x: 4, y: 4, z: 16, core: 2. Of those that a mesh axis runs over, the one named last changes fastest.
Arguments:
- fourier_slabs: bfloat16 [32768, 128, 128], P(('cls', 'pen')), may hold values from -6 to 6
- class_id: int32 [32768, 1], P(('cls', 'pen')), may hold values from 0 to 63; in each aligned block of 64 rows (0 to 63, 64 to 127, ...) at most 2 rows name the same one
- orientation: int32 [32768], P(('cls', 'pen')), may hold values from 0 to 127
- offset: bfloat16 [32768], P(('cls', 'pen')), may hold values from 0.099609375 to 0.8984375
- tomogram: int32 [32768], P(('cls', 'pen')), may hold values from 0 to 255
- defocus: bfloat16 [256], replicated, may hold values from 1 to 4
- class_map: bfloat16 [64, 128, 128, 128], P('cls', None, 'pen'), may hold values from -6 to 6
Outputs:
- class_gradient: float32 [64, 128, 128, 128], P('cls', 'pen')
The draws below stay inside these ranges and needn't reach their ends.
Inputs may be any that keep to these rules, and one draw needn't show every extreme that they name: `class_id`: in each aligned block of 64 rows (the particles of one device) no class is named by more than 2 rows, a bound that some block reaches.
All inputs are finite; a program needn't handle non-finite values.
Results may differ from the reference program's by a relative error of at most 0.0029.
Values may be sent and summed in bfloat16 or wider, within the bound.
A program may use at most 64 MiB of HBM per device.

```python
import math
import jax
import jax.numpy as jnp
import numpy as np
from jax import lax

X = 128
Y = 128
Z = 128
CLASSES = 64
P_DEV = 64
PARTICLES = 32768
CAP = 2
TOMOS = 256


def with_ends(array, stream_key, low, high):
    shape = array.shape
    spot = [jax.random.randint(jax.random.fold_in(stream_key, axis), (), 0, shape[axis]) for axis in range(len(shape))]
    array = array.at[tuple(spot)].set(low)
    longest = shape.index(max(shape))
    spot[longest] = (spot[longest] + 1) % shape[longest]
    return array.at[tuple(spot)].set(high)


def level_of(rng, dims, shards, least, largest):
    loudness, own = 1.0, jax.random.fold_in(rng, 6)
    for dim, parts in shards:
        steps = jnp.exp(jax.random.uniform(jax.random.fold_in(own, dim), (parts,), jnp.float32, least / len(shards), largest / len(shards)))
        loudness = loudness * jnp.repeat(steps, dims[dim] // parts).reshape([-1 if axis == dim else 1 for axis in range(len(dims))])
    return loudness


def deal_out(key, own, number, rows, amount, top, limit, skew):
    ranking = jax.random.permutation(key, amount)
    packed, common = shares(amount, rows * top, limit, skew, True), shares(amount, rows * top, limit, skew, False)
    places = jnp.arange(amount)

    def named(lengths, rotation):
        used = int((lengths > 0).sum())
        fixed = max(1, used // 4)
        passed = fixed + (places - fixed + rotation * (used - fixed)) % max(1, amount - fixed)
        return jnp.zeros((amount,), jnp.int32).at[ranking[jnp.where(places < fixed, places, passed)]].set(jnp.asarray(lengths, jnp.int32))

    lengths = jnp.where(number % 4 == 0, named(packed, number // 4), named(common, number - number // 4 - 1))
    mixed = jax.random.permutation(jax.random.fold_in(own, 3), amount)
    giver, sink = mixed[0:amount // 2 * 2:2], mixed[1:amount // 2 * 2:2]
    slack = jnp.minimum(lengths[giver] - 1, limit - lengths[sink]) // 2
    slack = jnp.where((giver == ranking[0]) | (sink == ranking[0]) | (lengths[sink] == 0), 0, jnp.maximum(slack, 0))
    passed = jax.random.randint(jax.random.fold_in(own, 4), (amount // 2,), 0, 1 << 20) % (slack + 1)
    lengths = lengths.at[giver].add(-passed).at[sink].add(passed)
    items = jnp.searchsorted(jnp.cumsum(lengths), jnp.arange(rows * top), side="right").astype(jnp.int32)
    table = items.reshape(top, rows).T
    table = table[jax.random.permutation(jax.random.fold_in(own, 1), rows)]
    rotation = jax.random.randint(jax.random.fold_in(own, 2), (rows, 1), 0, top)
    return jnp.take_along_axis(table, (jnp.arange(top)[None, :] + rotation) % top, axis=1)


def shares(number_of, total, reach, skew, full):
    portions = [(1 << 20) // math.isqrt(standing ** skew) + 1 for standing in range(1, number_of + 1)]
    largest = reach if full else min(reach, max(-(-total // number_of), total * portions[0] // sum(portions)))
    least = 1 if total - largest >= number_of - 1 else 0
    given, surplus = [largest] + [least] * (number_of - 1), total - largest - least * (number_of - 1)
    while surplus > 0:
        free = [i for i in range(1, number_of) if given[i] < largest] or [i for i in range(1, number_of) if given[i] < reach]
        mass, remaining = sum([portions[i] for i in free]), surplus
        for i in free:
            extra = min(reach - given[i], max(1, remaining * portions[i] // mass), surplus)
            given[i] = given[i] + extra
            surplus = surplus - extra
    return np.array(given)


def noise(rng, shape, deviation, bound, pieces=(), kind=jnp.bfloat16):
    array = deviation * jax.random.normal(rng, shape, jnp.float32)
    if pieces:
        array = array * level_of(rng, shape, pieces, -0.22, 0.18)
    return jnp.clip(array, -bound, bound).astype(kind)


def setup_inputs(seed: int = 0) -> dict:
    streams_of = jax.random.split(jax.random.key(seed), 8)
    fourier_slabs = noise(streams_of[0], (PARTICLES, Y, Z), 1.0, 6.0, ((0, 512),))
    class_id_keys = jax.random.split(jax.random.fold_in(streams_of[1], 1), PARTICLES // P_DEV)
    class_id_turns = jax.random.permutation(jax.random.fold_in(streams_of[1], 3), PARTICLES // P_DEV)
    class_id = jax.vmap(lambda own, number: deal_out(jax.random.fold_in(streams_of[1], 2), own, number, P_DEV, CLASSES, 1, CAP, 2))(class_id_keys, class_id_turns).reshape((PARTICLES, 1))
    orientation = with_ends(jax.random.randint(streams_of[2], (PARTICLES,), 0, X), jax.random.fold_in(streams_of[2], 1), 0, X - 1).astype(jnp.int32)
    offset = jnp.clip(0.099609375 + 0.7988281 * jax.random.uniform(streams_of[3], (PARTICLES,), jnp.float32) ** level_of(streams_of[3], (PARTICLES,), ((0, 512),), -0.2, 0.2), 0.099609375, 0.8984375).astype(jnp.bfloat16)
    tomogram = with_ends(jax.random.randint(streams_of[4], (PARTICLES,), 0, TOMOS), jax.random.fold_in(streams_of[4], 1), 0, TOMOS - 1).astype(jnp.int32)
    defocus = jnp.clip(jnp.exp(jax.random.uniform(streams_of[5], (TOMOS,), jnp.float32, math.log(1.0), math.log(4.0))), 1.0, 4.0).astype(jnp.bfloat16)
    class_map = noise(streams_of[6], (CLASSES, X, Y, Z), 1.0, 6.0, ((0, 32), (2, 16)))
    return {"fourier_slabs": fourier_slabs, "class_id": class_id, "orientation": orientation, "offset": offset, "tomogram": tomogram, "defocus": defocus, "class_map": class_map}


AMPLITUDE = 0.07
HIGHEST = lax.Precision.HIGHEST

def frequency(indices, extent):
    return jnp.where(indices < extent // 2, indices, indices - extent).astype(jnp.float32)

def hartley_table(extent):
    indices = jnp.arange(extent, dtype=jnp.int32)
    product = jnp.mod(indices[:, None] * indices[None, :], extent).astype(jnp.float32)
    angles = 2.0 * math.pi / extent * product
    return (jnp.cos(angles) + jnp.sin(angles)) / math.sqrt(extent)

def interp_kernel(position, extent):
    planes = jnp.arange(extent, dtype=jnp.float32)
    spacing = planes[:, None] - position[None, :]
    return jnp.sin(math.pi * spacing) * jnp.cos(math.pi * spacing / extent) / (extent * jnp.sin(math.pi * spacing / extent))

def contrast(focus_slot, shell_sq):
    phase_angle = math.pi * focus_slot[:, None] * shell_sq[None, :]
    return -(math.sqrt(1.0 - AMPLITUDE * AMPLITUDE) * jnp.sin(phase_angle) + AMPLITUDE * jnp.cos(phase_angle))

def slot_matches(class_ids, classes, capacity):
    labels = jnp.arange(classes, dtype=jnp.int32)
    member = (class_ids[:, None] == labels[None, :]).astype(jnp.int32)
    earlier = jnp.cumsum(member, axis=0) - member
    order_in = lax.optimization_barrier(jnp.sum(earlier * member, axis=1))
    slot_index = class_ids * capacity + order_in
    targets = jnp.arange(classes * capacity, dtype=jnp.int32)
    return (targets[:, None] == slot_index[None, :]).astype(jnp.int32)

def reference(fourier_slabs, class_id, orientation, offset, tomogram, defocus, class_map):
    voxels = Y * Z
    blocks = PARTICLES // P_DEV
    rows_freq = frequency(jnp.arange(Y, dtype=jnp.int32), Y)
    cols_freq = frequency(jnp.arange(Z, dtype=jnp.int32), Z)
    shell_sq = (((2.0 * rows_freq / Y) ** 2)[:, None] + ((2.0 * cols_freq / Z) ** 2)[None, :]).reshape(voxels)
    tomo_match = tomogram[:, None] == jnp.arange(TOMOS, dtype=jnp.int32)[None, :]
    focus_all = lax.optimization_barrier(jnp.sum(jnp.where(tomo_match, defocus.astype(jnp.float32)[None, :], jnp.float32(0.0)), axis=1))
    volumes = class_map.astype(jnp.float32).reshape(CLASSES, X, voxels)
    per_block = (fourier_slabs.reshape(blocks, P_DEV, voxels), class_id.reshape(blocks, P_DEV), orientation.astype(jnp.float32).reshape(blocks, P_DEV), offset.astype(jnp.float32).reshape(blocks, P_DEV), focus_all.reshape(blocks, P_DEV))

    def accumulate(running, block_data):
        block_slabs, block_ids, block_orient, block_offset, block_focus = block_data
        matches = slot_matches(block_ids, CLASSES, CAP)
        source = lax.optimization_barrier(jnp.sum(matches * jnp.arange(P_DEV, dtype=jnp.int32)[None, :], axis=1)).astype(jnp.int32)
        filled = lax.optimization_barrier(jnp.sum(matches, axis=1)).astype(jnp.float32)
        arrived_cells = jnp.take(block_slabs, source, axis=0).astype(jnp.float32) * filled[:, None]
        position = filled * (jnp.take(block_orient, source) + jnp.take(block_offset, source)) + 0.5 * (1.0 - filled)
        focus_slot = filled * jnp.take(block_focus, source)
        kernel = interp_kernel(position, X).astype(jnp.bfloat16)
        kernel = lax.optimization_barrier(kernel).astype(jnp.float32).reshape(X, CLASSES, CAP)
        predicted = jnp.einsum('xck,cxv->ckv', kernel, volumes, precision=HIGHEST)
        contrast_map = contrast(focus_slot, shell_sq).reshape(CLASSES, CAP, voxels)
        arrived_cells = arrived_cells.reshape(CLASSES, CAP, voxels)
        weighted = (filled.reshape(CLASSES, CAP, 1) * contrast_map * (arrived_cells - contrast_map * predicted)).astype(jnp.bfloat16)
        weighted = lax.optimization_barrier(weighted).astype(jnp.float32)
        return (running + jnp.einsum('xck,ckv->cxv', kernel, weighted, precision=HIGHEST), None)
    summed = lax.scan(accumulate, jnp.zeros((CLASSES, X, voxels), jnp.float32), per_block)[0]
    gradient = summed.reshape(CLASSES, X, Y, Z)
    along_z = jnp.einsum('cxyz,zk->cxyk', gradient, hartley_table(Z), precision=HIGHEST)
    along_x = jnp.einsum('kx,cxyz->ckyz', hartley_table(X), along_z, precision=HIGHEST)
    return jnp.einsum('ky,cxyz->cxkz', hartley_table(Y), along_x, precision=HIGHEST)
```

```python
import functools
import math

import jax
import jax.numpy as jnp
import numpy as np
from jax import lax
from jax.experimental import pallas as pl
from jax.experimental.pallas import tpu as pltpu
from jax.sharding import PartitionSpec as P

AMPLITUDE = 0.07
MESH = pl.DeviceIdType.MESH
F32 = jnp.float32
BF16 = jnp.bfloat16

EXTENT = 128
ZC = 16
PENS = 16
PART = 64
PLANE = PART * PENS
CHUNKS = 4
WIDE = 2 * EXTENT
POOL = 128
MAIN = 96


def power_series(function, degree, reach):
    nodes = np.cos(np.pi * (np.arange(degree + 1) + 0.5) / (degree + 1))
    nodes = 0.5 * reach * (nodes + 1.0)
    return [float(c) for c in np.polyfit(nodes, function(nodes), degree)[::-1]]


SIN_TURN = power_series(lambda s: 2 * np.pi * np.sinc(2 * np.sqrt(s)), 6, 0.25)
SIN_HALF = power_series(lambda s: np.pi * np.sinc(np.sqrt(s)), 5, 0.25)
COS_HALF = power_series(lambda s: np.cos(np.pi * np.sqrt(s)), 5, 0.25)
PHASE = math.asin(AMPLITUDE) / (2 * math.pi)


def horner(coefficients, x):
    total = coefficients[-1]
    for c in coefficients[-2::-1]:
        total = total * x + c
    return total


def hartley_tables():
    k = np.arange(EXTENT)
    angles = 2.0 * np.pi / EXTENT * ((k[:, None] * k[None, :]) % EXTENT)
    table = ((np.cos(angles) + np.sin(angles)) / math.sqrt(EXTENT)).astype(np.float32)
    high = table.astype(jnp.bfloat16)
    low = (table - high.astype(np.float32)).astype(jnp.bfloat16)
    return (
        np.concatenate([high, high, low], 0),
        np.concatenate([high, high, low], 1),
        np.concatenate([high, low], 1),
    )


def iota(shape, dim):
    return lax.broadcasted_iota(jnp.int32, shape, dim)


def dot(a, b):
    return jnp.dot(a, b, preferred_element_type=F32)


def dot_nt(a, b):
    return lax.dot_general(a, b, (((1,), (1,)), ((), ())), preferred_element_type=F32)


def split(a):
    high = a.astype(BF16)
    return high, (a - high.astype(F32)).astype(BF16)


def round_kernel(
    slots, first,
    lab_ref, slabs_ref, maps_ref, hz_ref, hx_ref, hy_ref,
    out_ref, most_ref,
    labp, p1, disp, labs, labr, send, recv, volume, kern, kern_t, focus, weighted,
    partial, partner, fs, fr, gather, flag_s, flag_r,
    lp_s, lp_r, p1_s, p1_r, own_s, cm_s, cm_r, cm_o, zl_s, zl_r, z_s, z_r, fl_s, fl_r, c_s, c_r, f_s, f_r,
):
    me = lax.axis_index("cls")
    pen = lax.axis_index("pen")
    z = me // 2
    core = lax.rem(me, 2)
    twin = (z * 2 + 1 - core, pen)

    def pen_at(o):
        return lax.rem(pen + o, PENS)

    def pen_from(o):
        return lax.rem(pen - o + PENS, PENS)

    def chip_at(o):
        return lax.rem(z + o, ZC)

    def chip_from(o):
        return lax.rem(z - o + ZC, ZC)

    def remote(src, dst, s, r, device):
        return pltpu.make_async_remote_copy(
            src_ref=src, dst_ref=dst, send_sem=s, recv_sem=r, device_id=device, device_id_type=MESH
        )

    def each(body, low=1, high=16):
        def step(i, carry):
            body(i)
            return carry

        lax.fori_loop(low, high, step, 0)

    barrier = pltpu.get_barrier_semaphore()

    def greet(o):
        pl.semaphore_signal(barrier, inc=1, device_id=(me, pen_at(o)), device_id_type=MESH)
        pl.semaphore_signal(barrier, inc=1, device_id=(chip_at(o) * 2 + core, pen), device_id_type=MESH)

    each(greet)
    pl.semaphore_signal(barrier, inc=1, device_id=twin, device_id_type=MESH)
    pl.semaphore_wait(barrier, 31)

    def lab_out(o):
        return remote(lab_ref, labp.at[pen], lp_s.at[o], lp_r.at[o], (me, pen_at(o)))

    def lab_in(o):
        return remote(lab_ref, labp.at[pen_from(o)], lp_s.at[o], lp_r.at[o], (me, pen_at(o)))

    def rows_out(j, o):
        to = pen_at(o)
        return remote(slabs_ref.at[to * CHUNKS + j], p1.at[j, pen], p1_s.at[j, o], p1_r.at[j, o], (me, to))

    def rows_in(j, o):
        to = pen_at(o)
        return remote(slabs_ref.at[to * CHUNKS + j], p1.at[j, pen_from(o)], p1_s.at[j, o], p1_r.at[j, o], (me, to))

    def rows_own(j):
        return pltpu.make_async_copy(slabs_ref.at[pen * CHUNKS + j], p1.at[j, pen], own_s.at[j])

    def map_out():
        return remote(maps_ref, volume.at[:, pl.ds(2 * core, 2)], cm_s, cm_r, twin)

    def map_in():
        return remote(maps_ref, volume.at[:, pl.ds(2 - 2 * core, 2)], cm_s, cm_r, twin)

    def map_own():
        return pltpu.make_async_copy(maps_ref, volume.at[:, pl.ds(2 * core, 2)], cm_o)

    def zlab_out(o):
        to = chip_at(o)
        return remote(labs.at[to], labr.at[z], zl_s.at[o], zl_r.at[o], (to * 2 + core, pen))

    def zlab_in(o):
        to = chip_at(o)
        return remote(labs.at[to], labr.at[chip_from(o)], zl_s.at[o], zl_r.at[o], (to * 2 + core, pen))

    def slot_out(j, o):
        to = chip_at(o)
        return remote(send.at[j, to], recv.at[j, z], z_s.at[j, o], z_r.at[j, o], (to * 2 + core, pen))

    def slot_in(j, o):
        to = chip_at(o)
        return remote(send.at[j, to], recv.at[j, chip_from(o)], z_s.at[j, o], z_r.at[j, o], (to * 2 + core, pen))

    def flag_copy():
        return remote(flag_s, flag_r, fl_s, fl_r, twin)

    def half_copy(j):
        return remote(partial.at[j, 1 - core], partner.at[j], c_s.at[j], c_r.at[j], twin)

    def cells_out(j, o):
        to = pen_at(o)
        return remote(fs.at[j, to], fr.at[j, pen], f_s.at[j, o], f_r.at[j, o], (me, to))

    def cells_in(j, o):
        to = pen_at(o)
        return remote(fs.at[j, to], fr.at[j, pen_from(o)], f_s.at[j, o], f_r.at[j, o], (me, to))

    each(lambda o: lab_out(o).start())
    for j in range(CHUNKS):
        each(lambda o, j=j: rows_out(j, o).start())
        rows_own(j).start()
    map_out().start()
    map_own().start()
    labp[pen] = lab_ref[...]
    labs[...] = jnp.zeros_like(labs)
    weighted[...] = jnp.zeros_like(weighted)

    each(lambda o: lab_in(o).wait_recv())
    fields = jnp.concatenate(
        [labp[2 * i].astype(F32) + labp[2 * i + 1].astype(F32) for i in range(PENS // 2)], axis=1
    )
    ids = fields[0:1]
    chip = jnp.floor(ids * 0.25)
    local = ids - 4.0 * chip + 1.0
    tri = jnp.where(iota((128, 128), 0) < iota((128, 128), 1), 1.0, 0.0).astype(BF16)
    running = jnp.zeros((ZC, 1), F32)
    ranks = []
    for i in range(PLANE // 128):
        part = chip[:, i * 128 : (i + 1) * 128]
        hot = jnp.where(iota((ZC, 128), 0).astype(F32) == part, 1.0, 0.0)
        before = dot(hot.astype(BF16), tri) + running
        ranks.append(jnp.sum(hot * before, axis=0, keepdims=True))
        running = running + jnp.sum(hot, axis=1, keepdims=True)
    most = jnp.max(running, axis=0, keepdims=True)
    rank = jnp.concatenate(ranks, axis=1) - float(first)
    rank = jnp.where((rank >= 0.0) & (rank < float(slots)), rank, -1.0)
    described = jnp.where(iota((16, PLANE), 0) == 0, local, fields).astype(BF16)
    row_of = iota((slots, PLANE), 0).astype(F32)

    def assign(d):
        here = jnp.where(chip == d.astype(F32), rank, -1.0)
        table = jnp.where(row_of == here, 1.0, 0.0).astype(BF16)
        disp[d] = table
        told = dot_nt(described, table)
        labs[d, :, 0:slots] = jnp.where(iota((16, slots), 0) == 4, most, told).astype(BF16)

    each(assign, 0, ZC)
    each(lambda o: zlab_out(o).start())
    labr[z] = labs[z]

    for j in range(CHUNKS):
        each(lambda o, j=j: rows_in(j, o).wait_recv())
        rows_own(j).wait()

        def pack(g, j=j):
            lines = p1[j].reshape(PLANE, WIDE)
            table = disp[pl.ds(g * 4, 4)].reshape(4 * slots, PLANE)
            send[j, pl.ds(g * 4, 4)] = dot(table, lines).astype(BF16).reshape(4, slots, WIDE)

        each(pack, 0, 4)
        each(lambda o, j=j: slot_out(j, o).start())
        recv[j, z] = send[j, z]

    each(lambda o: zlab_in(o).wait_recv())
    flag_s[...] = jnp.broadcast_to(
        jnp.max(jnp.max(labr[:, 4:5, :].astype(F32), axis=0), axis=1, keepdims=True), (16, 128)
    ).astype(BF16)
    flag_copy().start()

    def interpolate(s):
        info = labr[s].astype(F32)
        member = info[0:1]
        plane, fraction = info[1:2], info[2:3] + jnp.where(member == 0.0, 0.5, 0.0)
        x = iota((EXTENT, 128), 0).astype(F32)
        away = x - (plane + fraction)
        t = away * (1.0 / EXTENT)
        t = t - jnp.round(t)
        t2 = t * t
        both = x + plane
        sign = 2.0 * (both - 2.0 * jnp.floor(both * 0.5)) - 1.0
        centred = fraction - 0.5
        lift = horner(COS_HALF, centred * centred) * (1.0 / EXTENT)
        value = sign * lift * horner(COS_HALF, t2) / (t * horner(SIN_HALF, t2))
        turned = value.T
        members = jnp.broadcast_to(member, (EXTENT, 128))
        members_turned = members.T
        for q in range(4):
            kern_t[q * EXTENT : (q + 1) * EXTENT, pl.ds(pl.multiple_of(s * 128, 128), 128)] = jnp.where(
                members == q + 1.0, value, 0.0
            ).astype(BF16)
            kern[s, :, q * EXTENT : (q + 1) * EXTENT] = jnp.where(
                members_turned == q + 1.0, turned, 0.0
            ).astype(BF16)
        focus[s] = jnp.broadcast_to(info[3:4] * 0.5, (128, 128)).T

    each(interpolate, 0, ZC)
    map_in().wait_recv()
    map_own().wait()

    lane = iota((1, WIDE), 1)
    column = lane - jnp.where(lane >= EXTENT, EXTENT, 0)
    column = jnp.where(column < EXTENT // 2, column, column - EXTENT).astype(F32)
    for j in range(CHUNKS):
        row = pen * (2 * CHUNKS) + 2 * j + jnp.where(lane >= EXTENT, 1, 0)
        row = jnp.where(row < EXTENT // 2, row, row - EXTENT).astype(F32)
        shell = (2.0 / EXTENT * row) ** 2 + (2.0 / EXTENT * column) ** 2
        each(lambda o, j=j: slot_in(j, o).wait_recv())

        def weigh(s, j=j, shell=shell):
            predicted = dot(kern[s, 0:slots, :], volume[j].reshape(4 * EXTENT, WIDE))
            half = focus[s, 0:slots, :]
            turns = jnp.concatenate([half, half], axis=1) * shell + PHASE
            r = turns - jnp.round(turns)
            wave = r * horner(SIN_TURN, r * r)
            value = -wave * (recv[j, s].astype(F32) + wave * predicted)
            weighted[pl.ds(pl.multiple_of(s * 128, 128), slots), :] = value.astype(BF16)

        each(weigh, 0, ZC)
        partial[j] = dot(kern_t[...], weighted[...]).reshape(2, 2 * EXTENT, WIDE)
        half_copy(j).start()
        half_copy(j).wait_recv()
        mine = partial[j, core] + partner[j]
        high, low = split(mine)
        along_z = []
        for yy in range(2):
            cut = slice(yy * EXTENT, (yy + 1) * EXTENT)
            along_z.append(dot(jnp.concatenate([high[:, cut], low[:, cut], high[:, cut]], axis=1), hz_ref[...]))
        high, low = split(jnp.concatenate(along_z, axis=1))
        pieces = []
        for c in range(2):
            cut = slice(c * EXTENT, (c + 1) * EXTENT)
            along_x = dot(hx_ref[...], jnp.concatenate([high[cut], low[cut], high[cut]], axis=0))
            pieces.append(along_x.reshape(PENS, 8, WIDE))
        fs[j] = jnp.concatenate(pieces, axis=1).astype(BF16)
        each(lambda o, j=j: cells_out(j, o).start())
        fr[j, pen] = fs[j, pen]

    for j in range(CHUNKS):
        each(lambda o, j=j: cells_in(j, o).wait_recv())

        def place(r, j=j):
            for yy in range(2):
                gather[r * 8 + 2 * j + yy] = fr[j, r, :, yy * EXTENT : (yy + 1) * EXTENT].astype(F32)

        each(place, 0, PENS)
    for pair in range(8):
        cells = jnp.concatenate([gather[:, 2 * pair, :], gather[:, 2 * pair + 1, :]], axis=1).astype(BF16)
        along_y = dot(hy_ref[...], jnp.concatenate([cells, cells], axis=0))
        for i in range(2):
            c, kx = divmod(2 * pair + i, 8)
            out_ref[c, kx] = along_y[:, i * EXTENT : (i + 1) * EXTENT]

    flag_copy().wait()
    most_ref[...] = jnp.maximum(flag_s[0:8].astype(F32), flag_r[0:8].astype(F32))
    map_out().wait_send()
    each(lambda o: lab_out(o).wait_send())
    each(lambda o: zlab_out(o).wait_send())
    for j in range(CHUNKS):
        half_copy(j).wait_send()
        each(lambda o, j=j: rows_out(j, o).wait_send())
        each(lambda o, j=j: slot_out(j, o).wait_send())
        each(lambda o, j=j: cells_out(j, o).wait_send())


def one_round(slots, first, collective, lab, slabs, maps, tables):
    dma = pltpu.SemaphoreType.DMA
    vmem = pl.BlockSpec(memory_space=pltpu.VMEM)
    anywhere = pl.BlockSpec(memory_space=pl.ANY)
    return pl.pallas_call(
        functools.partial(round_kernel, slots, first),
        out_shape=[
            jax.ShapeDtypeStruct((2, 8, EXTENT, EXTENT), F32),
            jax.ShapeDtypeStruct((8, 128), F32),
        ],
        in_specs=[vmem, anywhere, anywhere, vmem, vmem, vmem],
        out_specs=[vmem, vmem],
        scratch_shapes=[
            pltpu.VMEM((PENS, 16, 128), BF16),
            pltpu.VMEM((CHUNKS, PENS, PART, WIDE), BF16),
            pltpu.VMEM((ZC, slots, PLANE), BF16),
            pltpu.VMEM((ZC, 16, 128), BF16),
            pltpu.VMEM((ZC, 16, 128), BF16),
            pltpu.VMEM((CHUNKS, ZC, slots, WIDE), BF16),
            pltpu.VMEM((CHUNKS, ZC, slots, WIDE), BF16),
            pltpu.VMEM((CHUNKS, 4, EXTENT, WIDE), BF16),
            pltpu.VMEM((ZC, 128, 4 * EXTENT), BF16),
            pltpu.VMEM((4 * EXTENT, ZC * 128), BF16),
            pltpu.VMEM((ZC, 128, 128), F32),
            pltpu.VMEM((ZC * 128, WIDE), BF16),
            pltpu.VMEM((CHUNKS, 2, 2 * EXTENT, WIDE), F32),
            pltpu.VMEM((CHUNKS, 2 * EXTENT, WIDE), F32),
            pltpu.VMEM((CHUNKS, PENS, 16, WIDE), BF16),
            pltpu.VMEM((CHUNKS, PENS, 16, WIDE), BF16),
            pltpu.VMEM((EXTENT, 16, EXTENT), F32),
            pltpu.VMEM((16, 128), BF16),
            pltpu.VMEM((16, 128), BF16),
            dma((16,)), dma((16,)), dma((CHUNKS, 16)), dma((CHUNKS, 16)), dma((CHUNKS,)),
            dma, dma, dma, dma((16,)), dma((16,)), dma((CHUNKS, 16)), dma((CHUNKS, 16)),
            dma, dma, dma((CHUNKS,)), dma((CHUNKS,)), dma((CHUNKS, 16)), dma((CHUNKS, 16)),
        ],
        compiler_params=pltpu.CompilerParams(
            collective_id=collective, has_side_effects=True, vmem_limit_bytes=48 << 20
        ),
        name=f"round_{collective}",
    )(lab, slabs, maps, *tables)


def per_device(fourier_slabs, class_id, orientation, offset, tomogram, defocus, class_map):
    tomo_match = tomogram[None, :] == jnp.arange(defocus.shape[0], dtype=jnp.int32)[:, None]
    focus_here = jnp.sum(jnp.where(tomo_match, defocus.astype(F32)[:, None], 0.0), axis=0)
    fields = jnp.stack(
        [class_id[:, 0].astype(F32), orientation.astype(F32), offset.astype(F32), focus_here]
    )
    twice = jnp.concatenate([fields, fields], axis=1)
    side = jnp.arange(2 * PART, dtype=jnp.int32)[None, :] // PART
    lab = jnp.where(side == lax.rem(lax.axis_index("pen"), 2), twice, 0.0)
    lab = jnp.pad(lab, ((0, 12), (0, 0))).astype(BF16)
    slabs = fourier_slabs.reshape(PART, PENS * CHUNKS, WIDE).transpose(1, 0, 2)
    maps = class_map.reshape(2, EXTENT, CHUNKS, WIDE).transpose(2, 0, 1, 3)
    tables = [jnp.asarray(t) for t in hartley_tables()]
    gradient, most = one_round(MAIN, 0, 0, lab, slabs, maps, tables)
    return lax.cond(
        most[0, 0] > MAIN,
        lambda g: g + one_round(POOL - MAIN, MAIN, 1, lab, slabs, maps, tables)[0],
        lambda g: g,
        gradient,
    )


def solution(mesh):
    in_specs = (
        P(("cls", "pen"), None, None),
        P(("cls", "pen"), None),
        P(("cls", "pen")),
        P(("cls", "pen")),
        P(("cls", "pen")),
        P(),
        P("cls", None, "pen", None),
    )
    return jax.shard_map(
        per_device, mesh=mesh, in_specs=in_specs, out_specs=P("cls", "pen", None, None), check_vma=False
    )
```

```python
import functools
import math

import jax
import jax.numpy as jnp
import numpy as np
from jax import lax
from jax.experimental import pallas as pl
from jax.experimental.pallas import tpu as pltpu
from jax.sharding import PartitionSpec as P

AMPLITUDE = 0.07
MESH = pl.DeviceIdType.MESH
F32 = jnp.float32
BF16 = jnp.bfloat16

EXTENT = 128
ZC = 16
PENS = 16
PART = 64
PLANE = PART * PENS
ROWS = 2
CHUNKS = 8 // ROWS
WIDE = ROWS * EXTENT
POOL = 128
MAIN = 96


def power_series(function, degree, reach):
    nodes = np.cos(np.pi * (np.arange(degree + 1) + 0.5) / (degree + 1))
    nodes = 0.5 * reach * (nodes + 1.0)
    return [float(c) for c in np.polyfit(nodes, function(nodes), degree)[::-1]]


SIN_TURN = power_series(lambda s: 2 * np.pi * np.sinc(2 * np.sqrt(s)), 6, 0.25)
SIN_HALF = power_series(lambda s: np.pi * np.sinc(np.sqrt(s)), 5, 0.25)
COS_HALF = power_series(lambda s: np.cos(np.pi * np.sqrt(s)), 5, 0.25)
PHASE = math.asin(AMPLITUDE) / (2 * math.pi)


def horner(coefficients, x):
    total = coefficients[-1]
    for c in coefficients[-2::-1]:
        total = total * x + c
    return total


def hartley_tables():
    k = np.arange(EXTENT)
    angles = 2.0 * np.pi / EXTENT * ((k[:, None] * k[None, :]) % EXTENT)
    table = ((np.cos(angles) + np.sin(angles)) / math.sqrt(EXTENT)).astype(np.float32)
    high = table.astype(jnp.bfloat16)
    low = (table - high.astype(np.float32)).astype(jnp.bfloat16)
    return (
        np.concatenate([high, high, low], 0),
        np.concatenate([high, high, low], 1),
        np.concatenate([high, low], 1),
    )


def iota(shape, dim):
    return lax.broadcasted_iota(jnp.int32, shape, dim)


def dot(a, b):
    return jnp.dot(a, b, preferred_element_type=F32)


def dot_nt(a, b):
    return lax.dot_general(a, b, (((1,), (1,)), ((), ())), preferred_element_type=F32)


def split(a):
    high = a.astype(BF16)
    return high, (a - high.astype(F32)).astype(BF16)


def abreast(parts):
    return parts[0] if len(parts) == 1 else jnp.concatenate(parts, axis=1)


def round_kernel(
    slots, first,
    ids_ref, plane_ref, offset_ref, tomo_ref, defocus_ref, slabs_ref, maps_ref, hz_ref, hx_ref, hy_ref,
    out_ref, most_ref,
    lab, labp, p1, disp, labs, labg, labr, send, recv, volume, kern, kern_t, focus, weighted,
    partial, partner, fs, fr, gather, flag_s, flag_r,
    lp_s, lp_r, p1_s, p1_r, own_s, cm_s, cm_r, cm_o, zl_s, zl_r, lb_s, lb_r, z_s, z_r, fl_s, fl_r, c_s, c_r, f_s, f_r,
):
    me = lax.axis_index("cls")
    pen = lax.axis_index("pen")
    z = me // 2
    core = lax.rem(me, 2)
    twin = (z * 2 + 1 - core, pen)

    def pen_at(o):
        return lax.rem(pen + o, PENS)

    def pen_from(o):
        return lax.rem(pen - o + PENS, PENS)

    def reach(i):
        half = (i + 1) // 2
        return lax.rem(half + lax.rem(i + 1, 2) * (ZC - 2 * half) + ZC, ZC)

    def chip_at(i):
        return lax.rem(z + reach(i), ZC)

    def chip_from(i):
        return lax.rem(z - reach(i) + ZC, ZC)

    def remote(src, dst, s, r, device):
        return pltpu.make_async_remote_copy(
            src_ref=src, dst_ref=dst, send_sem=s, recv_sem=r, device_id=device, device_id_type=MESH
        )

    def each(body, low=1, high=16):
        def step(i, carry):
            body(i)
            return carry

        lax.fori_loop(low, high, step, 0)

    barrier = pltpu.get_barrier_semaphore()

    def greet(o):
        pl.semaphore_signal(barrier, inc=1, device_id=(me, pen_at(o)), device_id_type=MESH)
        pl.semaphore_signal(barrier, inc=1, device_id=(chip_at(o) * 2 + core, pen), device_id_type=MESH)

    each(greet)
    pl.semaphore_signal(barrier, inc=1, device_id=twin, device_id_type=MESH)

    tomo_match = jnp.where(iota((256, PART), 0) == tomo_ref[...], 1.0, 0.0).astype(BF16)
    defocus = jnp.broadcast_to(defocus_ref[...].astype(F32), (8, 256)).astype(BF16)
    focus_here = dot(defocus, tomo_match)[0:1]
    line = iota((16, PART), 0)
    told = jnp.where(
        line == 0,
        ids_ref[...].astype(F32),
        jnp.where(
            line == 1,
            plane_ref[...].astype(F32),
            jnp.where(line == 2, offset_ref[...].astype(F32), jnp.where(line == 3, focus_here, 0.0)),
        ),
    )
    spot = iota((PART, 128), 0) + PART * lax.rem(pen, 2)
    spread = jnp.where(iota((PART, 128), 1) == spot, 1.0, 0.0).astype(BF16)
    lab[...] = dot(told.astype(BF16), spread).astype(BF16)
    labp[pen] = lab[...]
    labs[...] = jnp.zeros_like(labs)
    tri = jnp.where(iota((128, 128), 0) < iota((128, 128), 1), 1.0, 0.0).astype(BF16)

    pl.semaphore_wait(barrier, 31)

    def lab_out(o):
        return remote(lab, labp.at[pen], lp_s.at[o], lp_r.at[o], (me, pen_at(o)))

    def lab_in(o):
        return remote(lab, labp.at[pen_from(o)], lp_s.at[o], lp_r.at[o], (me, pen_at(o)))

    def rows_out(j, o):
        to = pen_at(o)
        return remote(slabs_ref.at[pl.ds(to * 8 + j * ROWS, ROWS)], p1.at[j, pen], p1_s.at[j, o], p1_r.at[j, o], (me, to))

    def rows_in(j, o):
        to = pen_at(o)
        return remote(slabs_ref.at[pl.ds(to * 8 + j * ROWS, ROWS)], p1.at[j, pen_from(o)], p1_s.at[j, o], p1_r.at[j, o], (me, to))

    def rows_own(j):
        return pltpu.make_async_copy(slabs_ref.at[pl.ds(pen * 8 + j * ROWS, ROWS)], p1.at[j, pen], own_s.at[j])

    def map_out():
        return remote(maps_ref, volume.at[:, pl.ds(2 * core, 2)], cm_s, cm_r, twin)

    def map_in():
        return remote(maps_ref, volume.at[:, pl.ds(2 - 2 * core, 2)], cm_s, cm_r, twin)

    def map_own():
        return pltpu.make_async_copy(maps_ref, volume.at[:, pl.ds(2 * core, 2)], cm_o)

    def zlab_out():
        o = lax.rem(pen - z + ZC, ZC)
        return remote(labs.at[pen], labg.at[z], zl_s, zl_r.at[o], (pen * 2 + core, pen))

    def zlab_in(o):
        source = lax.rem(z - o + ZC, ZC)
        return remote(labs.at[source], labg.at[source], zl_s, zl_r.at[o], (source * 2 + core, pen))

    def tell_out(o):
        return remote(labg, labr, lb_s.at[o], lb_r, (me, pen_at(o)))

    def tell_in():
        return remote(labg, labr, lb_s.at[0], lb_r, (me, z))

    def slot_out(j, i):
        to = chip_at(i)
        return remote(send.at[j, i], recv.at[j, i], z_s.at[j, i], z_r.at[j, i], (to * 2 + core, pen))

    def flag_copy():
        return remote(flag_s, flag_r, fl_s, fl_r, twin)

    def half_copy(j):
        return remote(partial.at[j, 1 - core], partner.at[j], c_s.at[j], c_r.at[j], twin)

    def cells_out(j, o):
        to = pen_at(o)
        return remote(fs.at[j, to], fr.at[j, pen], f_s.at[j, o], f_r.at[j, o], (me, to))

    def cells_in(j, o):
        to = pen_at(o)
        return remote(fs.at[j, to], fr.at[j, pen_from(o)], f_s.at[j, o], f_r.at[j, o], (me, to))

    def hand_out(j):
        each(lambda o: rows_out(j, o).start())
        rows_own(j).start()

    each(lambda o: lab_out(o).start())
    hand_out(0)
    hand_out(1)

    each(lambda o: lab_in(o).wait_recv())
    fields = jnp.concatenate(
        [labp[2 * i].astype(F32) + labp[2 * i + 1].astype(F32) for i in range(PENS // 2)], axis=1
    )
    ids = fields[0:1]
    chip = jnp.floor(ids * 0.25)
    local = ids - 4.0 * chip + 1.0
    running = jnp.zeros((ZC, 1), F32)
    ranks = []
    for i in range(PLANE // 128):
        part = chip[:, i * 128 : (i + 1) * 128]
        hot = jnp.where(iota((ZC, 128), 0).astype(F32) == part, 1.0, 0.0)
        before = dot(hot.astype(BF16), tri) + running
        ranks.append(jnp.sum(hot * before, axis=0, keepdims=True))
        running = running + jnp.sum(hot, axis=1, keepdims=True)
    most = jnp.max(running, axis=0, keepdims=True)
    rank = jnp.concatenate(ranks, axis=1) - float(first)
    rank = jnp.where((rank >= 0.0) & (rank < float(slots)), rank, -1.0)
    described = jnp.where(iota((16, PLANE), 0) == 0, local, fields).astype(BF16)
    row_of = iota((slots, PLANE), 0).astype(F32)

    def assign(d):
        here = jnp.where(chip == d.astype(F32), rank, -1.0)
        disp[d] = jnp.where(row_of == here, 1.0, 0.0).astype(BF16)

    def describe(d):
        held = dot_nt(described, disp[d])
        labs[d, :, 0:slots] = jnp.where(iota((16, slots), 0) == 4, most, held).astype(BF16)

    def pack(j):
        each(lambda o: rows_in(j, o).wait_recv())
        rows_own(j).wait()

        def some(g):
            table = jnp.concatenate([disp[chip_at(4 * g + k)] for k in range(4)], axis=0)
            lines = abreast([p1[j, :, r].reshape(PLANE, EXTENT) for r in range(ROWS)])
            send[j, pl.ds(g * 4, 4)] = dot(table, lines).astype(BF16).reshape(4, slots, WIDE)
            each(lambda i: slot_out(j, i).start(), jnp.maximum(4 * g, 1), 4 * g + 4)

        each(some, 0, 4)
        recv[j, 0] = send[j, 0]

    each(assign, 0, ZC)
    pack(0)
    each(hand_out, 2, min(4, CHUNKS))
    pack(1)
    each(describe, 0, ZC)

    @pl.when(pen != z)
    def _():
        zlab_out().start()

    map_out().start()
    map_own().start()
    each(hand_out, 4, CHUNKS)
    each(pack, 2, CHUNKS)

    @pl.when(pen == z)
    def _():
        labg[z] = labs[z]
        each(lambda o: zlab_in(o).wait_recv())
        each(lambda o: tell_out(o).start())
        labr[...] = labg[...]

    @pl.when(pen != z)
    def _():
        tell_in().wait_recv()

    flag_s[...] = jnp.broadcast_to(
        jnp.max(jnp.max(labr[:, 4:5, :].astype(F32), axis=0), axis=1, keepdims=True), (16, 128)
    ).astype(BF16)
    flag_copy().start()

    def interpolate(g):
        for k in range(4):
            i = 4 * g + k
            info = labr[chip_from(i)].astype(F32)
            member = info[0:1]
            plane, fraction = info[1:2], info[2:3] + jnp.where(member == 0.0, 0.5, 0.0)
            x = iota((EXTENT, 128), 0).astype(F32)
            away = x - (plane + fraction)
            t = away * (1.0 / EXTENT)
            t = t - jnp.round(t)
            t2 = t * t
            both = x + plane
            sign = 2.0 * (both - 2.0 * jnp.floor(both * 0.5)) - 1.0
            centred = fraction - 0.5
            lift = horner(COS_HALF, centred * centred) * (1.0 / EXTENT)
            value = sign * lift * horner(COS_HALF, t2) / (t * horner(SIN_HALF, t2))
            turned = value.T
            members = jnp.broadcast_to(member, (EXTENT, 128))
            members_turned = members.T
            for q in range(4):
                cut = slice(q * EXTENT, (q + 1) * EXTENT)
                kern_t[g, cut, k * 128 : (k + 1) * 128] = jnp.where(members == q + 1.0, value, 0.0).astype(BF16)
                kern[i, :, cut] = jnp.where(members_turned == q + 1.0, turned, 0.0).astype(BF16)
            focus[i] = jnp.broadcast_to(info[3:4] * 0.5, (128, 128)).T

    each(interpolate, 0, 4)
    weighted[...] = jnp.zeros_like(weighted)
    map_in().wait_recv()
    map_own().wait()

    column = iota((1, EXTENT), 1)
    column = jnp.where(column < EXTENT // 2, column, column - EXTENT).astype(F32)

    def place(j):
        each(lambda o: cells_in(j, o).wait_recv())

        def one(r):
            for k in range(ROWS):
                gather[r * 8 + j * ROWS + k] = fr[j, r, :, k * EXTENT : (k + 1) * EXTENT].astype(F32)

        each(one, 0, PENS)

    def work(j):
        shells = []
        for k in range(ROWS):
            row = jnp.full((1, EXTENT), pen * 8 + j * ROWS + k, jnp.int32)
            row = jnp.where(row < EXTENT // 2, row, row - EXTENT).astype(F32)
            shells.append((2.0 / EXTENT * row) ** 2 + (2.0 / EXTENT * column) ** 2)
        shell = abreast(shells)

        def weigh(i):
            @pl.when(i > 0)
            def _():
                slot_out(j, i).wait_recv()

            maps = abreast([volume[j * ROWS + k].reshape(4 * EXTENT, EXTENT) for k in range(ROWS)])
            predicted = dot(kern[i, 0:slots, :], maps)
            turns = abreast([focus[i, 0:slots, :]] * ROWS) * shell + PHASE
            r = turns - jnp.round(turns)
            wave = r * horner(SIN_TURN, r * r)
            value = -wave * (recv[j, i].astype(F32) + wave * predicted)
            weighted[pl.ds(pl.multiple_of(i * 128, 128), slots), :] = value.astype(BF16)

        total = None
        for g in range(4):
            each(weigh, 4 * g, 4 * g + 4)
            term = dot(kern_t[g], weighted[g * 512 : (g + 1) * 512, :])
            total = term if total is None else total + term
        partial[j] = total.reshape(2, 2 * EXTENT, WIDE)
        half_copy(j).start()

        @pl.when(j > 0)
        def _():
            finish(j - 1)

        @pl.when(j > 1)
        def _():
            place(j - 2)

    def finish(j):
        half_copy(j).wait_recv()
        mine = partial[j, core] + partner[j]
        high, low = split(mine)
        along_z = []
        for k in range(ROWS):
            cut = slice(k * EXTENT, (k + 1) * EXTENT)
            along_z.append(dot(abreast([high[:, cut], low[:, cut], high[:, cut]]), hz_ref[...]))
        high, low = split(abreast(along_z))
        pieces = []
        for c in range(2):
            cut = slice(c * EXTENT, (c + 1) * EXTENT)
            along_x = dot(hx_ref[...], jnp.concatenate([high[cut], low[cut], high[cut]], axis=0))
            pieces.append(along_x.reshape(PENS, 8, WIDE))
        fs[j] = jnp.concatenate(pieces, axis=1).astype(BF16)
        each(lambda o: cells_out(j, o).start())
        fr[j, pen] = fs[j, pen]

    each(work, 0, CHUNKS)
    finish(CHUNKS - 1)
    place(CHUNKS - 2)
    place(CHUNKS - 1)
    for pair in range(8):
        cells = jnp.concatenate([gather[:, 2 * pair, :], gather[:, 2 * pair + 1, :]], axis=1).astype(BF16)
        along_y = dot(hy_ref[...], jnp.concatenate([cells, cells], axis=0))
        for i in range(2):
            c, kx = divmod(2 * pair + i, 8)
            out_ref[c, kx] = along_y[:, i * EXTENT : (i + 1) * EXTENT]

    flag_copy().wait()
    most_ref[...] = jnp.maximum(flag_s[0:8].astype(F32), flag_r[0:8].astype(F32))
    map_out().wait_send()
    each(lambda o: lab_out(o).wait_send())

    @pl.when(pen != z)
    def _():
        zlab_out().wait_send()

    @pl.when(pen == z)
    def _():
        each(lambda o: tell_out(o).wait_send())

    def drain(j):
        half_copy(j).wait_send()
        each(lambda o: rows_out(j, o).wait_send())
        each(lambda i: slot_out(j, i).wait_send())
        each(lambda o: cells_out(j, o).wait_send())

    each(drain, 0, CHUNKS)


def one_round(slots, first, collective, operands, tables):
    dma = pltpu.SemaphoreType.DMA
    vmem = pl.BlockSpec(memory_space=pltpu.VMEM)
    anywhere = pl.BlockSpec(memory_space=pl.ANY)
    return pl.pallas_call(
        functools.partial(round_kernel, slots, first),
        out_shape=[
            jax.ShapeDtypeStruct((2, 8, EXTENT, EXTENT), F32),
            jax.ShapeDtypeStruct((8, 128), F32),
        ],
        in_specs=[vmem] * 5 + [anywhere] * 2 + [vmem] * 3,
        out_specs=[vmem, vmem],
        scratch_shapes=[
            pltpu.VMEM((16, 128), BF16),
            pltpu.VMEM((PENS, 16, 128), BF16),
            pltpu.VMEM((CHUNKS, PENS, ROWS, PART, EXTENT), BF16),
            pltpu.VMEM((ZC, slots, PLANE), BF16),
            pltpu.VMEM((ZC, 16, 128), BF16),
            pltpu.VMEM((ZC, 16, 128), BF16),
            pltpu.VMEM((ZC, 16, 128), BF16),
            pltpu.VMEM((CHUNKS, ZC, slots, WIDE), BF16),
            pltpu.VMEM((CHUNKS, ZC, slots, WIDE), BF16),
            pltpu.VMEM((8, 4, EXTENT, EXTENT), BF16),
            pltpu.VMEM((ZC, 128, 4 * EXTENT), BF16),
            pltpu.VMEM((4, 4 * EXTENT, 512), BF16),
            pltpu.VMEM((ZC, 128, 128), F32),
            pltpu.VMEM((ZC * 128, WIDE), BF16),
            pltpu.VMEM((CHUNKS, 2, 2 * EXTENT, WIDE), F32),
            pltpu.VMEM((CHUNKS, 2 * EXTENT, WIDE), F32),
            pltpu.VMEM((CHUNKS, PENS, 16, WIDE), BF16),
            pltpu.VMEM((CHUNKS, PENS, 16, WIDE), BF16),
            pltpu.VMEM((EXTENT, 16, EXTENT), F32),
            pltpu.VMEM((16, 128), BF16),
            pltpu.VMEM((16, 128), BF16),
            dma((16,)), dma((16,)), dma((CHUNKS, 16)), dma((CHUNKS, 16)), dma((CHUNKS,)),
            dma, dma, dma, dma, dma((16,)), dma((16,)), dma, dma((CHUNKS, 16)), dma((CHUNKS, 16)),
            dma, dma, dma((CHUNKS,)), dma((CHUNKS,)), dma((CHUNKS, 16)), dma((CHUNKS, 16)),
        ],
        compiler_params=pltpu.CompilerParams(
            collective_id=collective, has_side_effects=True, vmem_limit_bytes=48 << 20
        ),
        name=f"round_{collective}",
    )(*operands, *tables)


def per_device(fourier_slabs, class_id, orientation, offset, tomogram, defocus, class_map):
    operands = [
        class_id.reshape(1, PART),
        orientation.reshape(1, PART),
        offset.reshape(1, PART),
        tomogram.reshape(1, PART),
        defocus.reshape(1, 256),
        fourier_slabs.transpose(1, 0, 2),
        class_map.transpose(2, 0, 1, 3),
    ]
    tables = [jnp.asarray(t) for t in hartley_tables()]
    gradient, most = one_round(MAIN, 0, 0, operands, tables)
    return lax.cond(
        most[0, 0] > MAIN,
        lambda g: g + one_round(POOL - MAIN, MAIN, 1, operands, tables)[0],
        lambda g: g,
        gradient,
    )


def solution(mesh):
    in_specs = (
        P(("cls", "pen"), None, None),
        P(("cls", "pen"), None),
        P(("cls", "pen")),
        P(("cls", "pen")),
        P(("cls", "pen")),
        P(),
        P("cls", None, "pen", None),
    )
    return jax.shard_map(
        per_device, mesh=mesh, in_specs=in_specs, out_specs=P("cls", "pen", None, None), check_vma=False
    )
```

```python
import functools
import math

import jax
import jax.numpy as jnp
import numpy as np
from jax import lax
from jax.experimental import pallas as pl
from jax.experimental.pallas import tpu as pltpu
from jax.sharding import PartitionSpec as P

AMPLITUDE = 0.07
MESH = pl.DeviceIdType.MESH
F32 = jnp.float32
BF16 = jnp.bfloat16

EXTENT = 128
ZC = 16
PENS = 16
PART = 64
PLANE = PART * PENS
ROWS = 2
CHUNKS = 8 // ROWS
WIDE = ROWS * EXTENT
POOL = 128
MAIN = 96


def power_series(function, degree, reach):
    nodes = np.cos(np.pi * (np.arange(degree + 1) + 0.5) / (degree + 1))
    nodes = 0.5 * reach * (nodes + 1.0)
    return [float(c) for c in np.polyfit(nodes, function(nodes), degree)[::-1]]


SIN_TURN = power_series(lambda s: 2 * np.pi * np.sinc(2 * np.sqrt(s)), 6, 0.25)
SIN_HALF = power_series(lambda s: np.pi * np.sinc(np.sqrt(s)), 5, 0.25)
COS_HALF = power_series(lambda s: np.cos(np.pi * np.sqrt(s)), 5, 0.25)
PHASE = math.asin(AMPLITUDE) / (2 * math.pi)


def horner(coefficients, x):
    total = coefficients[-1]
    for c in coefficients[-2::-1]:
        total = total * x + c
    return total


def hartley_tables():
    k = np.arange(EXTENT)
    angles = 2.0 * np.pi / EXTENT * ((k[:, None] * k[None, :]) % EXTENT)
    table = ((np.cos(angles) + np.sin(angles)) / math.sqrt(EXTENT)).astype(np.float32)
    high = table.astype(jnp.bfloat16)
    low = (table - high.astype(np.float32)).astype(jnp.bfloat16)
    return (
        np.concatenate([high, high, low], 0),
        np.concatenate([high, high, low], 1),
        np.concatenate([high, low], 1),
    )


def iota(shape, dim):
    return lax.broadcasted_iota(jnp.int32, shape, dim)


def dot(a, b):
    return jnp.dot(a, b, preferred_element_type=F32)


def dot_nt(a, b):
    return lax.dot_general(a, b, (((1,), (1,)), ((), ())), preferred_element_type=F32)


def split(a):
    high = a.astype(BF16)
    return high, (a - high.astype(F32)).astype(BF16)


def abreast(parts):
    return parts[0] if len(parts) == 1 else jnp.concatenate(parts, axis=1)


def round_kernel(
    slots, first,
    ids_ref, plane_ref, offset_ref, tomo_ref, defocus_ref, slabs_ref, maps_ref, hz_ref, hx_ref, hy_ref,
    out_ref, most_ref,
    lab, labp, p1, disp, labs, labg, labr, send, recv, spaced, volume, kern, kern_t, focus, weighted,
    partial, partner, fs, fr, gather, flag_s, flag_r,
    lp_s, lp_r, p1_s, p1_r, own_s, cm_s, cm_r, zl_s, zl_r, lb_s, lb_r, z_s, z_r, fl_s, fl_r, c_s, c_r, f_s, f_r,
):
    me = lax.axis_index("cls")
    pen = lax.axis_index("pen")
    z = me // 2
    core = lax.rem(me, 2)
    twin = (z * 2 + 1 - core, pen)

    def pen_at(o):
        return lax.rem(pen + o, PENS)

    def pen_from(o):
        return lax.rem(pen - o + PENS, PENS)

    def reach(i):
        half = (i + 1) // 2
        return lax.rem(half + lax.rem(i + 1, 2) * (ZC - 2 * half) + ZC, ZC)

    def chip_at(i):
        return lax.rem(z + reach(i), ZC)

    def chip_from(i):
        return lax.rem(z - reach(i) + ZC, ZC)

    def remote(src, dst, s, r, device):
        return pltpu.make_async_remote_copy(
            src_ref=src, dst_ref=dst, send_sem=s, recv_sem=r, device_id=device, device_id_type=MESH
        )

    def each(body, low=1, high=16):
        def step(i, carry):
            body(i)
            return carry

        lax.fori_loop(low, high, step, 0)

    barrier = pltpu.get_barrier_semaphore()

    def greet(o):
        pl.semaphore_signal(barrier, inc=1, device_id=(me, pen_at(o)), device_id_type=MESH)
        pl.semaphore_signal(barrier, inc=1, device_id=(chip_at(o) * 2 + core, pen), device_id_type=MESH)

    each(greet)
    pl.semaphore_signal(barrier, inc=1, device_id=twin, device_id_type=MESH)

    tomo_match = jnp.where(iota((256, PART), 0) == tomo_ref[...], 1.0, 0.0).astype(BF16)
    defocus = defocus_ref[...].astype(F32)
    first_half = jnp.broadcast_to(defocus[0:1], (8, 128)).astype(BF16)
    last_half = jnp.broadcast_to(defocus[1:2], (8, 128)).astype(BF16)
    focus_here = (dot(first_half, tomo_match[0:128]) + dot(last_half, tomo_match[128:256]))[0:1]
    line = iota((16, PART), 0)
    told = jnp.where(
        line == 0,
        ids_ref[...].astype(F32),
        jnp.where(
            line == 1,
            plane_ref[...].astype(F32),
            jnp.where(line == 2, offset_ref[...].astype(F32), jnp.where(line == 3, focus_here, 0.0)),
        ),
    )
    spot = iota((PART, 128), 0) + PART * lax.rem(pen, 2)
    spread = jnp.where(iota((PART, 128), 1) == spot, 1.0, 0.0).astype(BF16)
    lab[...] = dot(told.astype(BF16), spread).astype(BF16)
    labp[pen] = lab[...]
    labs[...] = jnp.zeros_like(labs)
    tri = jnp.where(iota((128, 128), 0) < iota((128, 128), 1), 1.0, 0.0).astype(BF16)

    pl.semaphore_wait(barrier, 31)

    def lab_out(o):
        return remote(lab, labp.at[pen], lp_s.at[o], lp_r.at[o], (me, pen_at(o)))

    def lab_in(o):
        return remote(lab, labp.at[pen_from(o)], lp_s.at[o], lp_r.at[o], (me, pen_at(o)))

    def rows_out(j, o):
        to = pen_at(o)
        return remote(slabs_ref.at[pl.ds(to * 8 + j * ROWS, ROWS)], p1.at[j, pen], p1_s.at[j, o], p1_r.at[j, o], (me, to))

    def rows_in(j, o):
        to = pen_at(o)
        return remote(slabs_ref.at[pl.ds(to * 8 + j * ROWS, ROWS)], p1.at[j, pen_from(o)], p1_s.at[j, o], p1_r.at[j, o], (me, to))

    def rows_own(j):
        return pltpu.make_async_copy(slabs_ref.at[pl.ds(pen * 8 + j * ROWS, ROWS)], p1.at[j, pen], own_s.at[j])

    def map_out():
        mine = volume.at[:, pl.ds(2 * core, 2)]
        return remote(mine, mine, cm_s, cm_r, twin)

    def map_in():
        other = volume.at[:, pl.ds(2 - 2 * core, 2)]
        return remote(other, other, cm_s, cm_r, twin)

    def zlab_out():
        o = lax.rem(pen - z + ZC, ZC)
        return remote(labs.at[pen], labg.at[z], zl_s, zl_r.at[o], (pen * 2 + core, pen))

    def zlab_in(o):
        source = lax.rem(z - o + ZC, ZC)
        return remote(labs.at[source], labg.at[source], zl_s, zl_r.at[o], (source * 2 + core, pen))

    def tell_out(o):
        return remote(labg, labr, lb_s.at[o], lb_r, (me, pen_at(o)))

    def tell_in():
        return remote(labg, labr, lb_s.at[0], lb_r, (me, z))

    def slot_out(j, i):
        to = chip_at(i)
        return remote(send.at[j, i], recv.at[j, i], z_s.at[j, i], z_r.at[j, i], (to * 2 + core, pen))

    def flag_copy():
        return remote(flag_s, flag_r, fl_s, fl_r, twin)

    def half_copy(j):
        return remote(partial.at[j, 1 - core], partner.at[j], c_s.at[j], c_r.at[j], twin)

    def cells_out(j, o):
        to = pen_at(o)
        return remote(fs.at[j, to], fr.at[j, pen], f_s.at[j, o], f_r.at[j, o], (me, to))

    def cells_in(j, o):
        to = pen_at(o)
        return remote(fs.at[j, to], fr.at[j, pen_from(o)], f_s.at[j, o], f_r.at[j, o], (me, to))

    def hand_out(j):
        each(lambda o: rows_out(j, o).start())
        rows_own(j).start()

    each(lambda o: lab_out(o).start())
    hand_out(0)
    hand_out(1)

    each(lambda o: lab_in(o).wait_recv())
    fields = jnp.concatenate(
        [labp[2 * i].astype(F32) + labp[2 * i + 1].astype(F32) for i in range(PENS // 2)], axis=1
    )
    ids = fields[0:1]
    chip = jnp.floor(ids * 0.25)
    local = ids - 4.0 * chip + 1.0
    running = jnp.zeros((ZC, 1), F32)
    ranks = []
    for i in range(PLANE // 128):
        part = chip[:, i * 128 : (i + 1) * 128]
        hot = jnp.where(iota((ZC, 128), 0).astype(F32) == part, 1.0, 0.0)
        before = dot(hot.astype(BF16), tri) + running
        ranks.append(jnp.sum(hot * before, axis=0, keepdims=True))
        running = running + jnp.sum(hot, axis=1, keepdims=True)
    most = jnp.max(running, axis=0, keepdims=True)
    rank = jnp.concatenate(ranks, axis=1) - float(first)
    rank = jnp.where((rank >= 0.0) & (rank < float(slots)), rank, -1.0)
    described = jnp.where(iota((16, PLANE), 0) == 0, local, fields).astype(BF16)
    row_of = iota((slots, PLANE), 0).astype(F32)

    def assign(d):
        here = jnp.where(chip == d.astype(F32), rank, -1.0)
        disp[d] = jnp.where(row_of == here, 1.0, 0.0).astype(BF16)

    def describe(d):
        held = dot_nt(described, disp[d])
        labs[d, :, 0:slots] = jnp.where(iota((16, slots), 0) == 4, most, held).astype(BF16)

    def pack(j):
        each(lambda o: rows_in(j, o).wait_recv())
        rows_own(j).wait()

        def some(g):
            table = jnp.concatenate([disp[chip_at(4 * g + k)] for k in range(4)], axis=0)
            lines = abreast([p1[j, :, r].reshape(PLANE, EXTENT) for r in range(ROWS)])
            send[j, pl.ds(g * 4, 4)] = dot(table, lines).astype(BF16).reshape(4, slots, WIDE)
            each(lambda i: slot_out(j, i).start(), jnp.maximum(4 * g, 1), 4 * g + 4)

        each(some, 0, 4)
        recv[j, 0] = send[j, 0]

    each(assign, 0, ZC)
    pack(0)
    each(hand_out, 2, min(4, CHUNKS))
    pack(1)
    each(describe, 0, ZC)

    @pl.when(pen != z)
    def _():
        zlab_out().start()

    spaced[...] = maps_ref[...].reshape(2 * EXTENT, 8, EXTENT).astype(F32)
    for y in range(8):
        volume[y, pl.ds(2 * core, 2)] = spaced[:, y, :].astype(BF16).reshape(2, EXTENT, EXTENT)
    map_out().start()
    each(hand_out, 4, CHUNKS)
    each(pack, 2, CHUNKS)

    @pl.when(pen == z)
    def _():
        labg[z] = labs[z]
        each(lambda o: zlab_in(o).wait_recv())
        each(lambda o: tell_out(o).start())
        labr[...] = labg[...]

    @pl.when(pen != z)
    def _():
        tell_in().wait_recv()

    flag_s[...] = jnp.broadcast_to(
        jnp.max(jnp.max(labr[:, 4:5, :].astype(F32), axis=0), axis=1, keepdims=True), (16, 128)
    ).astype(BF16)
    flag_copy().start()

    def interpolate(g):
        for k in range(4):
            i = 4 * g + k
            info = labr[chip_from(i)].astype(F32)
            member = info[0:1]
            plane, fraction = info[1:2], info[2:3] + jnp.where(member == 0.0, 0.5, 0.0)
            x = iota((EXTENT, 128), 0).astype(F32)
            away = x - (plane + fraction)
            t = away * (1.0 / EXTENT)
            t = t - jnp.round(t)
            t2 = t * t
            both = x + plane
            sign = 2.0 * (both - 2.0 * jnp.floor(both * 0.5)) - 1.0
            centred = fraction - 0.5
            lift = horner(COS_HALF, centred * centred) * (1.0 / EXTENT)
            value = sign * lift * horner(COS_HALF, t2) / (t * horner(SIN_HALF, t2))
            turned = value.T
            members = jnp.broadcast_to(member, (EXTENT, 128))
            members_turned = members.T
            for q in range(4):
                cut = slice(q * EXTENT, (q + 1) * EXTENT)
                kern_t[g, cut, k * 128 : (k + 1) * 128] = jnp.where(members == q + 1.0, value, 0.0).astype(BF16)
                kern[i, :, cut] = jnp.where(members_turned == q + 1.0, turned, 0.0).astype(BF16)
            focus[i] = jnp.broadcast_to(info[3:4] * 0.5, (128, 128)).T

    each(interpolate, 0, 4)
    weighted[...] = jnp.zeros_like(weighted)
    map_in().wait_recv()

    column = iota((1, EXTENT), 1)
    column = jnp.where(column < EXTENT // 2, column, column - EXTENT).astype(F32)

    def place(j):
        each(lambda o: cells_in(j, o).wait_recv())

        def one(r):
            for k in range(ROWS):
                gather[r * 8 + j * ROWS + k] = fr[j, r, :, k * EXTENT : (k + 1) * EXTENT].astype(F32)

        each(one, 0, PENS)

    def work(j):
        shells = []
        for k in range(ROWS):
            row = jnp.full((1, EXTENT), pen * 8 + j * ROWS + k, jnp.int32)
            row = jnp.where(row < EXTENT // 2, row, row - EXTENT).astype(F32)
            shells.append((2.0 / EXTENT * row) ** 2 + (2.0 / EXTENT * column) ** 2)
        shell = abreast(shells)

        def weigh(i):
            @pl.when(i > 0)
            def _():
                slot_out(j, i).wait_recv()

            maps = abreast([volume[j * ROWS + k].reshape(4 * EXTENT, EXTENT) for k in range(ROWS)])
            predicted = dot(kern[i, 0:slots, :], maps)
            turns = abreast([focus[i, 0:slots, :]] * ROWS) * shell + PHASE
            r = turns - jnp.round(turns)
            wave = r * horner(SIN_TURN, r * r)
            value = -wave * (recv[j, i].astype(F32) + wave * predicted)
            weighted[pl.ds(pl.multiple_of(i * 128, 128), slots), :] = value.astype(BF16)

        total = None
        for g in range(4):
            each(weigh, 4 * g, 4 * g + 4)
            term = dot(kern_t[g], weighted[g * 512 : (g + 1) * 512, :])
            total = term if total is None else total + term
        partial[j] = total.reshape(2, 2 * EXTENT, WIDE)
        half_copy(j).start()

        @pl.when(j > 0)
        def _():
            finish(j - 1)

        @pl.when(j > 1)
        def _():
            place(j - 2)

    def finish(j):
        half_copy(j).wait_recv()
        mine = partial[j, core] + partner[j]
        high, low = split(mine)
        along_z = []
        for k in range(ROWS):
            cut = slice(k * EXTENT, (k + 1) * EXTENT)
            along_z.append(dot(abreast([high[:, cut], low[:, cut], high[:, cut]]), hz_ref[...]))
        high, low = split(abreast(along_z))
        pieces = []
        for c in range(2):
            cut = slice(c * EXTENT, (c + 1) * EXTENT)
            along_x = dot(hx_ref[...], jnp.concatenate([high[cut], low[cut], high[cut]], axis=0))
            pieces.append(along_x.reshape(PENS, 8, WIDE))
        fs[j] = jnp.concatenate(pieces, axis=1).astype(BF16)
        each(lambda o: cells_out(j, o).start())
        fr[j, pen] = fs[j, pen]

    each(work, 0, CHUNKS)
    finish(CHUNKS - 1)
    place(CHUNKS - 2)
    place(CHUNKS - 1)
    for pair in range(8):
        cells = jnp.concatenate([gather[:, 2 * pair, :], gather[:, 2 * pair + 1, :]], axis=1).astype(BF16)
        along_y = dot(hy_ref[...], jnp.concatenate([cells, cells], axis=0))
        for i in range(2):
            c, kx = divmod(2 * pair + i, 8)
            out_ref[c, kx] = along_y[:, i * EXTENT : (i + 1) * EXTENT]

    flag_copy().wait()
    most_ref[...] = jnp.maximum(flag_s[0:8].astype(F32), flag_r[0:8].astype(F32))
    map_out().wait_send()
    each(lambda o: lab_out(o).wait_send())

    @pl.when(pen != z)
    def _():
        zlab_out().wait_send()

    @pl.when(pen == z)
    def _():
        each(lambda o: tell_out(o).wait_send())

    def drain(j):
        half_copy(j).wait_send()
        each(lambda o: rows_out(j, o).wait_send())
        each(lambda i: slot_out(j, i).wait_send())
        each(lambda o: cells_out(j, o).wait_send())

    each(drain, 0, CHUNKS)


def one_round(slots, first, collective, operands, tables):
    dma = pltpu.SemaphoreType.DMA
    vmem = pl.BlockSpec(memory_space=pltpu.VMEM)
    anywhere = pl.BlockSpec(memory_space=pl.ANY)
    return pl.pallas_call(
        functools.partial(round_kernel, slots, first),
        out_shape=[
            jax.ShapeDtypeStruct((2, 8, EXTENT, EXTENT), F32),
            jax.ShapeDtypeStruct((8, 128), F32),
        ],
        in_specs=[vmem] * 5 + [anywhere] + [vmem] * 4,
        out_specs=[vmem, vmem],
        scratch_shapes=[
            pltpu.VMEM((16, 128), BF16),
            pltpu.VMEM((PENS, 16, 128), BF16),
            pltpu.VMEM((CHUNKS, PENS, ROWS, PART, EXTENT), BF16),
            pltpu.VMEM((ZC, slots, PLANE), BF16),
            pltpu.VMEM((ZC, 16, 128), BF16),
            pltpu.VMEM((ZC, 16, 128), BF16),
            pltpu.VMEM((ZC, 16, 128), BF16),
            pltpu.VMEM((CHUNKS, ZC, slots, WIDE), BF16),
            pltpu.VMEM((CHUNKS, ZC, slots, WIDE), BF16),
            pltpu.VMEM((2 * EXTENT, 8, EXTENT), F32),
            pltpu.VMEM((8, 4, EXTENT, EXTENT), BF16),
            pltpu.VMEM((ZC, 128, 4 * EXTENT), BF16),
            pltpu.VMEM((4, 4 * EXTENT, 512), BF16),
            pltpu.VMEM((ZC, 128, 128), F32),
            pltpu.VMEM((ZC * 128, WIDE), BF16),
            pltpu.VMEM((CHUNKS, 2, 2 * EXTENT, WIDE), F32),
            pltpu.VMEM((CHUNKS, 2 * EXTENT, WIDE), F32),
            pltpu.VMEM((CHUNKS, PENS, 16, WIDE), BF16),
            pltpu.VMEM((CHUNKS, PENS, 16, WIDE), BF16),
            pltpu.VMEM((EXTENT, 16, EXTENT), F32),
            pltpu.VMEM((16, 128), BF16),
            pltpu.VMEM((16, 128), BF16),
            dma((16,)), dma((16,)), dma((CHUNKS, 16)), dma((CHUNKS, 16)), dma((CHUNKS,)),
            dma, dma, dma, dma((16,)), dma((16,)), dma, dma((CHUNKS, 16)), dma((CHUNKS, 16)),
            dma, dma, dma((CHUNKS,)), dma((CHUNKS,)), dma((CHUNKS, 16)), dma((CHUNKS, 16)),
        ],
        compiler_params=pltpu.CompilerParams(
            collective_id=collective, has_side_effects=True, vmem_limit_bytes=48 << 20
        ),
        name=f"round_{collective}",
    )(*operands, *tables)


def per_device(fourier_slabs, class_id, orientation, offset, tomogram, defocus, class_map):
    operands = [
        class_id.reshape(1, PART),
        orientation.reshape(1, PART),
        offset.reshape(1, PART),
        tomogram.reshape(1, PART),
        defocus.reshape(2, 128),
        fourier_slabs.transpose(1, 0, 2),
        class_map,
    ]
    tables = [jnp.asarray(t) for t in hartley_tables()]
    gradient, most = one_round(MAIN, 0, 0, operands, tables)
    return lax.cond(
        most[0, 0] > MAIN,
        lambda g: g + one_round(POOL - MAIN, MAIN, 1, operands, tables)[0],
        lambda g: g,
        gradient,
    )


def solution(mesh):
    in_specs = (
        P(("cls", "pen"), None, None),
        P(("cls", "pen"), None),
        P(("cls", "pen")),
        P(("cls", "pen")),
        P(("cls", "pen")),
        P(),
        P("cls", None, "pen", None),
    )
    return jax.shard_map(
        per_device, mesh=mesh, in_specs=in_specs, out_specs=P("cls", "pen", None, None), check_vma=False
    )
```
